32 devices in a mesh: grp: 4 (over z), dev: 8 (over y, x, core).
Axes of the slice: x: 2, y: 2, z: 4, core: 2. Of those that a mesh axis runs over, the one named last changes fastest.
Arguments:
- positions: float32 [3, 32768], P(None, ('grp', 'dev')), may hold values from -3 to 3
- velocities: float32 [3, 32768], P(None, ('grp', 'dev')), may hold values from -5 to 5
- accelerations: float32 [3, 32768], P(None, ('grp', 'dev')), may hold values from -3 to 3
- jerks: float32 [3, 32768], P(None, ('grp', 'dev')), may hold values from -3 to 3
- levels: int32 [32768], P(('grp', 'dev')), may hold values from 0 to 5
- counts: int32 [2, 32], replicated, may hold values from 1 to 256, 4096 in all within a row
- active_rows: int32 [2, 8192], P(None, ('grp', 'dev')), may hold values from 0 to 1023, as said below
Outputs:
- new_positions: float32 [3, 32768], P(None, ('grp', 'dev'))
- new_velocities: float32 [3, 32768], P(None, ('grp', 'dev'))
- new_accelerations: float32 [3, 32768], P(None, ('grp', 'dev'))
- new_jerks: float32 [3, 32768], P(None, ('grp', 'dev'))
The draws below stay inside these ranges and needn't reach their ends.
Inputs may be any that keep to these rules, and one draw needn't show every extreme that they name: In each step the 32 counts sum to exactly 4096 and the largest of them is exactly 256. `active_rows`: for each step and device, the 256 entries of the device's slots are distinct indices of that device's own stars; only the first counts of them are live.
All inputs are finite; a program needn't handle non-finite values.
Results may differ from the reference program's by a relative error of at most 0.00022.
Values sent between devices are 32-bit elements; how exact they have to be, the bound alone decides.
A program may use at most 128 MiB of HBM per device.

```python
import math
import jax
import jax.numpy as jnp
import numpy as np
from jax import lax

STAR_DEV = 1024
ACT_CAP = 256
STEPS = 2
LEVELS = 6
STARS = 32768
ACTIVE = 4096
DEVICES = 32


def draw_active_rows(key, part):
    keys = jax.random.split(jax.random.fold_in(key, 7), STEPS * DEVICES)
    chosen = jax.vmap(lambda single: jax.random.permutation(single, STAR_DEV)[:ACT_CAP])(keys)
    return chosen.reshape(STEPS, DEVICES * ACT_CAP).astype(jnp.int32)


def place_ends(entries, key, low, top_value):
    dims = entries.shape
    spot = [jax.random.randint(jax.random.fold_in(key, axis), (), 0, dims[axis]) for axis in range(len(dims))]
    entries = entries.at[tuple(spot)].set(low)
    longest = dims.index(max(dims))
    spot[longest] = (spot[longest] + 1) % dims[longest]
    return entries.at[tuple(spot)].set(top_value)


def steps_of(stream_key, extent, cuts, low, top_value):
    loudness = 1.0
    for axis_at, shards_of in cuts:
        heights = jax.random.uniform(jax.random.fold_in(jax.random.fold_in(stream_key, 6), axis_at), (shards_of,), jnp.float32, low / len(cuts), top_value / len(cuts))
        loudness = loudness * jnp.repeat(jnp.exp(heights), extent[axis_at] // shards_of).reshape((-1,) + (1,) * (len(extent) - 1 - axis_at))
    return loudness


def length_profile(amount, total, limit, slope):
    portions = [(1 << 20) // math.isqrt(grade ** slope) + 1 for grade in range(2, amount + 1)]
    spare, given = total - limit - (amount - 1), [1] * (amount - 1)
    while spare > 0:
        candidates = [i for i in range(amount - 1) if given[i] < limit]
        whole, budget = sum([portions[i] for i in candidates]), spare
        for i in candidates:
            more = min(limit - given[i], max(1, budget * portions[i] // whole), spare)
            given[i] = given[i] + more
            spare = spare - more
    return np.array([limit] + given)


def uneven_parts(stream_key, count, total, most, lean):
    if count == 2:
        one = jax.random.randint(stream_key, (), max(1, total - most), min(most, total - 1) + 1)
        return jnp.stack([one, total - one])
    tallies = jnp.asarray(length_profile(count, total, most, lean), jnp.int32)
    couples = (count - 1) // 2
    source_of, taker = tallies[1:1 + 2 * couples:2], tallies[2:2 + 2 * couples:2]
    room = jnp.minimum(source_of - 1, most - taker)
    passed = jax.random.randint(jax.random.fold_in(stream_key, 1), (couples,), 0, 1 << 20) % (room + 1)
    tallies = tallies.at[1:1 + 2 * couples:2].set(source_of - passed).at[2:2 + 2 * couples:2].set(taker + passed)
    return tallies[jax.random.permutation(jax.random.fold_in(stream_key, 2), count)]


def scatter_about(key, dims, width, limit, shards=(), kind=jnp.bfloat16):
    result = width * jax.random.normal(key, dims, jnp.float32)
    if shards:
        result = result * steps_of(key, dims, shards, -0.22, 0.18)
    return jnp.clip(result, -limit, limit).astype(kind)


def setup_inputs(seed: int = 0) -> dict:
    splits = jax.random.split(jax.random.key(seed), 8)
    positions = scatter_about(splits[0], (3, STARS), 0.5, 3.0, ((1, 32),), jnp.float32)
    velocities = scatter_about(splits[1], (3, STARS), 1.0, 5.0, ((1, 32),), jnp.float32)
    accelerations = scatter_about(splits[2], (3, STARS), 0.5, 3.0, ((1, 32),), jnp.float32)
    jerks = scatter_about(splits[3], (3, STARS), 0.5, 3.0, ((1, 32),), jnp.float32)
    levels = place_ends(jax.random.randint(splits[4], (STARS,), 0, LEVELS), jax.random.fold_in(splits[4], 1), 0, LEVELS - 1).astype(jnp.int32)
    counts = jax.vmap(lambda own: uneven_parts(own, DEVICES, ACTIVE, ACT_CAP, 2))(jax.random.split(splits[5], STEPS)).reshape((STEPS, DEVICES)).astype(jnp.int32)
    active_rows = draw_active_rows(jax.random.fold_in(splits[7], 71), 0)
    return dict(positions=positions, velocities=velocities, accelerations=accelerations, jerks=jerks, levels=levels, counts=counts, active_rows=active_rows)


tick_length = 1.0 / 128.0

def pair_block(targets, src_pos, src_vel, mass, soft_sq):
    gap_x = src_pos[0][None, :] - targets[0][:, None]
    gap_y = src_pos[1][None, :] - targets[1][:, None]
    gap_z = src_pos[2][None, :] - targets[2][:, None]
    drift_x = src_vel[0][None, :] - targets[3][:, None]
    drift_y = src_vel[1][None, :] - targets[4][:, None]
    drift_z = src_vel[2][None, :] - targets[5][:, None]
    squared = gap_x * gap_x + gap_y * gap_y + gap_z * gap_z + soft_sq
    inverse = lax.rsqrt(squared)
    weight = mass * inverse * inverse * inverse
    along = 3.0 * (gap_x * drift_x + gap_y * drift_y + gap_z * drift_z) * inverse * inverse
    return jnp.stack([lax.optimization_barrier(jnp.sum(weight * gap_x, axis=1)), lax.optimization_barrier(jnp.sum(weight * gap_y, axis=1)), lax.optimization_barrier(jnp.sum(weight * gap_z, axis=1)), lax.optimization_barrier(jnp.sum(weight * (drift_x - along * gap_x), axis=1)), lax.optimization_barrier(jnp.sum(weight * (drift_y - along * gap_y), axis=1)), lax.optimization_barrier(jnp.sum(weight * (drift_z - along * gap_z), axis=1))])

def predict(positions, velocities, accelerations, jerks, elapsed):
    span = elapsed[None, :]
    pred_pos = positions + span * velocities + 0.5 * span * span * accelerations + span * span * span / 6.0 * jerks
    pred_vel = velocities + span * accelerations + 0.5 * span * span * jerks
    return (pred_pos, pred_vel)

def correct(old_pos, old_vel, old_acc, old_jerk, force, jerk_new, span):
    span = span[None, :]
    new_vel = old_vel + 0.5 * span * (old_acc + force) + span * span / 12.0 * (old_jerk - jerk_new)
    new_pos = old_pos + 0.5 * span * (old_vel + new_vel) + span * span / 12.0 * (old_acc - force)
    return (new_pos, new_vel)

def reference(positions, velocities, accelerations, jerks, levels, counts, active_rows):
    mass = 1.0 / STARS
    soft_sq = 0.0004 * (131072.0 / STARS) ** (2.0 / 3.0)
    last_time = -(jnp.left_shift(jnp.int32(1), levels) - 1).astype(jnp.float32) * tick_length
    for step in range(STEPS):
        now = (step + 1) * tick_length
        pred_pos, pred_vel = predict(positions, velocities, accelerations, jerks, now - last_time)
        step_counts = counts[step]
        inclusive = jnp.cumsum(step_counts).astype(jnp.int32)
        first = (inclusive - step_counts).astype(jnp.int32)
        place = jnp.arange(ACTIVE, dtype=jnp.int32)
        owner = lax.optimization_barrier(jnp.sum((inclusive[None, :] <= place[:, None]).astype(jnp.int32), axis=1)).astype(jnp.int32)
        slot = (owner * ACT_CAP + place - first[owner]).astype(jnp.int32)
        ident = (owner * STAR_DEV + active_rows[step][slot]).astype(jnp.int32)
        targets = jnp.concatenate([pred_pos[:, ident], pred_vel[:, ident]], axis=0)
        block = math.gcd(ACTIVE, 64)
        grouped = targets.reshape(6, ACTIVE // block, block).transpose(1, 0, 2)
        sums = lax.map(lambda part_rows: pair_block(part_rows, pred_pos, pred_vel, mass, soft_sq), grouped)
        sums = sums.transpose(1, 0, 2).reshape(6, ACTIVE)
        span = now - last_time[ident]
        new_pos, new_vel = correct(positions[:, ident], velocities[:, ident], accelerations[:, ident], jerks[:, ident], sums[:3], sums[3:], span)
        positions = positions.at[:, ident].set(new_pos)
        velocities = velocities.at[:, ident].set(new_vel)
        accelerations = accelerations.at[:, ident].set(sums[:3])
        jerks = jerks.at[:, ident].set(sums[3:])
        last_time = last_time.at[ident].set(now)
    return (positions, velocities, accelerations, jerks)
```

```python
import functools

import jax
import jax.numpy as jnp
from jax import lax
from jax.experimental import pallas as pl
from jax.experimental.pallas import tpu as pltpu
from jax.sharding import PartitionSpec as P

tick_length = 1.0 / 128.0
COLS = 256
ROWS = 128
F32 = jnp.float32
BF16 = jnp.bfloat16
NT = (((1,), (1,)), ((), ()))


def split3(value):
    high = value.astype(BF16).astype(F32)
    rest = value - high
    middle = rest.astype(BF16).astype(F32)
    return high, middle, rest - middle


def accumulate(chunk, width, slots, left_ref, place_ref, pairs_ref, total_ref):
    for start in range(0, width, COLS):
        source = chunk[:, start : start + COLS]
        high, middle, low = split3(source)
        right = jnp.concatenate([high, high, high, middle, middle, low], axis=0).astype(BF16)
        parts = jnp.concatenate([high, middle, low, jnp.zeros_like(low)], axis=0).astype(BF16)
        for row in range(0, slots, ROWS):
            rows = slice(row, row + ROWS)
            mixed = jnp.dot(left_ref[rows, :], right, preferred_element_type=F32)
            for lane in range(0, COLS, 128):
                lanes = slice(lane, lane + 128)
                gap_x = source[0:1, lanes] - place_ref[0, rows, :]
                gap_y = source[1:2, lanes] - place_ref[1, rows, :]
                gap_z = source[2:3, lanes] - place_ref[2, rows, :]
                squared = gap_x * gap_x + gap_y * gap_y + gap_z * gap_z + place_ref[3, 0:1, :]
                inverse = lax.rsqrt(squared)
                twice = inverse * inverse
                weight = twice * inverse
                along = weight * twice * mixed[:, lanes]
                weight_high = weight.astype(BF16)
                along_high = along.astype(BF16)
                pairs_ref[0, rows, lanes] = weight_high
                pairs_ref[1, rows, lanes] = (weight - weight_high.astype(F32)).astype(BF16)
                pairs_ref[2, rows, lanes] = along_high
                pairs_ref[3, rows, lanes] = (along - along_high.astype(F32)).astype(BF16)
        total_ref[0:32, :] += lax.dot_general(
            parts, pairs_ref[0], NT, preferred_element_type=F32
        ) + lax.dot_general(parts, pairs_ref[1], NT, preferred_element_type=F32)
        total_ref[32:64, :] += lax.dot_general(
            parts, pairs_ref[2], NT, preferred_element_type=F32
        ) + lax.dot_general(parts, pairs_ref[3], NT, preferred_element_type=F32)


def kernel(
    groups,
    peers,
    steps,
    soft_sq,
    mass,
    positions,
    velocities,
    accelerations,
    jerks,
    levels,
    counts,
    active_rows,
    out_pos,
    out_vel,
    out_acc,
    out_jerk,
    held,
    state,
    picked,
    left,
    place,
    pairs,
    total,
    send_sem,
    recv_sem,
):
    stars = positions.shape[1]
    slots = active_rows.shape[1]
    grp = lax.axis_index("grp")
    dev = lax.axis_index("dev")
    me = grp * peers + dev

    barrier = pltpu.get_barrier_semaphore()
    for ahead in range(1, groups):
        pl.semaphore_signal(
            barrier, inc=1, device_id=(lax.rem(grp + ahead, groups), dev),
            device_id_type=pl.DeviceIdType.MESH,
        )
    for ahead in range(1, peers):
        pl.semaphore_signal(
            barrier, inc=1, device_id=(grp, lax.rem(dev + ahead, peers)),
            device_id_type=pl.DeviceIdType.MESH,
        )

    state[0:3, :] = positions[...]
    state[3:6, :] = velocities[...]
    state[6:9, :] = accelerations[...]
    state[9:12, :] = jerks[...]
    state[12:13, :] = -(jnp.left_shift(jnp.int32(1), levels[...]) - 1).astype(F32) * tick_length
    state[13:16, :] = jnp.zeros((3, stars), F32)
    place[3] = jnp.full((slots, 128), soft_sq, F32)

    def send(step, owner, lane, target):
        return pltpu.make_async_remote_copy(
            src_ref=held.at[step, owner],
            dst_ref=held.at[step, owner],
            send_sem=send_sem.at[step, lane],
            recv_sem=recv_sem.at[step, owner],
            device_id=target,
            device_id_type=pl.DeviceIdType.MESH,
        )

    def group_copy(step, ahead):
        return send(step, me, ahead - 1, (lax.rem(grp + ahead, groups), dev))

    def peer_copy(step, back, ahead):
        owner = lax.rem(grp + groups - back, groups) * peers + dev
        lane = (groups - 1) + back * (peers - 1) + ahead - 1
        return send(step, owner, lane, (grp, lax.rem(dev + ahead, peers)))

    def one_step(step, carry):
        now = (step + 1).astype(F32) * tick_length
        span = now - state[12:13, :]
        pred_pos = (
            state[0:3, :]
            + span * state[3:6, :]
            + 0.5 * span * span * state[6:9, :]
            + span * span * span / 6.0 * state[9:12, :]
        )
        pred_vel = state[3:6, :] + span * state[6:9, :] + 0.5 * span * span * state[9:12, :]
        held[step, me, 0:3, :] = pred_pos
        held[step, me, 3:6, :] = pred_vel
        held[step, me, 6:7, :] = jnp.sum(pred_pos * pred_vel, axis=0, keepdims=True)
        held[step, me, 7:8, :] = jnp.ones((1, stars), F32)

        @pl.when(step == 0)
        def _():
            pl.semaphore_wait(barrier, groups + peers - 2)

        for ahead in range(1, groups):
            group_copy(step, ahead).start()
        for ahead in range(1, peers):
            peer_copy(step, 0, ahead).start()

        rows = active_rows[pl.ds(step, 1), :]
        chosen = lax.broadcasted_iota(jnp.int32, (stars, slots), 0) == rows
        chosen = jnp.where(chosen, 1.0, 0.0).astype(BF16)
        values = jnp.concatenate([held[step, me], state[...]], axis=0)
        pieces = jnp.concatenate(split3(values), axis=0).astype(BF16)
        found = jnp.dot(pieces, chosen, preferred_element_type=F32)
        found = found[0:24] + (found[24:48] + found[48:72])
        picked[...] = found
        moved = jnp.concatenate(
            [-found[3:6], -found[0:3], jnp.ones((1, slots), F32), found[6:7]], axis=0
        )
        high, middle, low = split3(moved)
        side = jnp.concatenate(
            [high, middle, low, high, middle, high, found[0:8], jnp.zeros((72, slots), F32)], axis=0
        ).T
        left[...] = side[:, 0:48].astype(BF16)
        for axis in range(3):
            place[axis] = jnp.broadcast_to(side[:, 48 + axis : 49 + axis], (slots, 128))
        total[...] = jnp.zeros_like(total)

        def one_chunk(turn, inner):
            owner_grp = lax.rem(grp + groups - lax.rem(turn, groups), groups)
            owner_dev = lax.rem(dev + peers - turn // groups, peers)
            owner = owner_grp * peers + owner_dev

            @pl.when(turn == 1)
            def _():
                for back in range(1, groups):
                    sender = lax.rem(grp + groups - back, groups) * peers + dev
                    send(step, sender, 0, (grp, lax.rem(dev + 1, peers))).wait_recv()
                    for ahead in range(1, peers):
                        peer_copy(step, back, ahead).start()

            @pl.when(turn >= groups)
            def _():
                send(step, owner, 0, (grp, lax.rem(dev + 1, peers))).wait_recv()

            accumulate(held[step, owner], stars, slots, left, place, pairs, total)
            return inner

        lax.fori_loop(0, groups * peers, one_chunk, 0)

        for ahead in range(1, groups):
            group_copy(step, ahead).wait_send()
        for back in range(groups):
            for ahead in range(1, peers):
                peer_copy(step, back, ahead).wait_send()

        sums = total[...]
        direct = sums[0:8] + (sums[8:16] + sums[16:24])
        turned = sums[32:40] + (sums[40:48] + sums[48:56])
        pred = picked[0:8, :]
        force = mass * (direct[0:3] - pred[0:3] * direct[7:8])
        jerk = mass * (
            (direct[3:6] - pred[3:6] * direct[7:8]) - 3.0 * (turned[0:3] - pred[0:3] * turned[7:8])
        )
        old_pos, old_vel = picked[8:11, :], picked[11:14, :]
        old_acc, old_jerk = picked[14:17, :], picked[17:20, :]
        gone = now - picked[20:21, :]
        new_vel = old_vel + 0.5 * gone * (old_acc + force) + gone * gone / 12.0 * (old_jerk - jerk)
        new_pos = old_pos + 0.5 * gone * (old_vel + new_vel) + gone * gone / 12.0 * (old_acc - force)
        picked[0:3, :] = new_pos
        picked[3:6, :] = new_vel
        picked[6:9, :] = force
        picked[9:12, :] = jerk
        picked[12:13, :] = jnp.full((1, slots), now, F32)
        picked[13:14, :] = jnp.ones((1, slots), F32)
        picked[14:16, :] = jnp.zeros((2, slots), F32)
        live = lax.broadcasted_iota(jnp.int32, (1, slots), 1) < counts[step, me]
        pieces = jnp.concatenate(split3(jnp.where(live, picked[0:16, :], 0.0)), axis=0).astype(BF16)
        spread = lax.dot_general(pieces, chosen, NT, preferred_element_type=F32)
        spread = spread[0:16] + (spread[16:32] + spread[32:48])
        state[...] = jnp.where(spread[13:14] > 0.5, spread, state[...])
        return carry

    lax.fori_loop(0, steps, one_step, 0)
    out_pos[...] = state[0:3, :]
    out_vel[...] = state[3:6, :]
    out_acc[...] = state[6:9, :]
    out_jerk[...] = state[9:12, :]


def shards(groups, peers, positions, velocities, accelerations, jerks, levels, counts, active_rows):
    stars = positions.shape[1]
    steps, slots = active_rows.shape
    everyone = groups * peers
    stars_all = stars * everyone
    sends = (groups - 1) + groups * (peers - 1)
    vmem = pl.BlockSpec(memory_space=pltpu.VMEM)
    pairs_all = steps * slots * stars_all
    return pl.pallas_call(
        functools.partial(
            kernel,
            groups,
            peers,
            steps,
            0.0004 * (131072.0 / stars_all) ** (2.0 / 3.0),
            1.0 / stars_all,
        ),
        out_shape=[jax.ShapeDtypeStruct((3, stars), F32)] * 4,
        in_specs=[vmem] * 5 + [pl.BlockSpec(memory_space=pltpu.SMEM), vmem],
        out_specs=[vmem] * 4,
        scratch_shapes=[
            pltpu.VMEM((steps, everyone, 8, stars), F32),
            pltpu.VMEM((16, stars), F32),
            pltpu.VMEM((24, slots), F32),
            pltpu.VMEM((slots, 48), BF16),
            pltpu.VMEM((4, slots, 128), F32),
            pltpu.VMEM((4, slots, COLS), BF16),
            pltpu.VMEM((64, slots), F32),
            pltpu.SemaphoreType.DMA((steps, sends)),
            pltpu.SemaphoreType.DMA((steps, everyone)),
        ],
        compiler_params=pltpu.CompilerParams(
            collective_id=0, has_side_effects=True, vmem_limit_bytes=32 * 1024 * 1024
        ),
        cost_estimate=pl.CostEstimate(
            flops=40 * pairs_all, bytes_accessed=64 * stars, transcendentals=pairs_all
        ),
    )(positions, velocities, accelerations, jerks, levels[None, :], counts, active_rows)


def solution(mesh):
    split = P(None, ("grp", "dev"))
    return jax.shard_map(
        functools.partial(shards, mesh.shape["grp"], mesh.shape["dev"]),
        mesh=mesh,
        in_specs=(split, split, split, split, P(("grp", "dev")), P(), split),
        out_specs=(split, split, split, split),
        check_vma=False,
    )
```

```python
import functools

import jax
import jax.numpy as jnp
from jax import lax
from jax.experimental import pallas as pl
from jax.experimental.pallas import tpu as pltpu
from jax.sharding import PartitionSpec as P

tick_length = 1.0 / 128.0
COLS = 256
F32 = jnp.float32
BF16 = jnp.bfloat16
NT = (((1,), (1,)), ((), ()))


def split3(value):
    high = value.astype(BF16).astype(F32)
    rest = value - high
    middle = rest.astype(BF16).astype(F32)
    return high, middle, rest - middle


def accumulate(chunk, width, left_ref, place_ref, total_ref):
    high, middle, low = split3(chunk)
    right = jnp.concatenate([high, high, high, middle, middle, low], axis=0).astype(BF16)
    parts = jnp.concatenate([high, middle, low, jnp.zeros_like(low)], axis=0).astype(BF16)
    direct = total_ref[0:32, :]
    turned = total_ref[32:64, :]
    for start in range(0, width, COLS):
        columns = slice(start, start + COLS)
        mixed = jnp.dot(left_ref[...], right[:, columns], preferred_element_type=F32)
        pieces = [[], [], [], []]
        for lane in range(0, COLS, 128):
            lanes = slice(start + lane, start + lane + 128)
            gap_x = chunk[0:1, lanes] - place_ref[0]
            gap_y = chunk[1:2, lanes] - place_ref[1]
            gap_z = chunk[2:3, lanes] - place_ref[2]
            squared = gap_x * gap_x + gap_y * gap_y + gap_z * gap_z + place_ref[3, 0:1, :]
            inverse = lax.rsqrt(squared)
            twice = inverse * inverse
            weight = twice * inverse
            along = weight * twice * mixed[:, lane : lane + 128]
            weight_high = weight.astype(BF16)
            along_high = along.astype(BF16)
            pieces[0].append(weight_high)
            pieces[1].append((weight - weight_high.astype(F32)).astype(BF16))
            pieces[2].append(along_high)
            pieces[3].append((along - along_high.astype(F32)).astype(BF16))
        part = parts[:, columns]
        sums = [
            lax.dot_general(part, jnp.concatenate(piece, axis=1), NT, preferred_element_type=F32)
            for piece in pieces
        ]
        direct = direct + sums[0] + sums[1]
        turned = turned + sums[2] + sums[3]
    total_ref[0:32, :] = direct
    total_ref[32:64, :] = turned


def kernel(
    groups,
    peers,
    steps,
    soft_sq,
    mass,
    positions,
    velocities,
    accelerations,
    jerks,
    levels,
    counts,
    active_rows,
    out_pos,
    out_vel,
    out_acc,
    out_jerk,
    held,
    state,
    picked,
    left,
    place,
    total,
    send_sem,
    recv_sem,
):
    stars = positions.shape[1]
    slots = active_rows.shape[1]
    grp = lax.axis_index("grp")
    dev = lax.axis_index("dev")
    me = grp * peers + dev

    barrier = pltpu.get_barrier_semaphore()
    for ahead in range(1, groups):
        pl.semaphore_signal(
            barrier, inc=1, device_id=(lax.rem(grp + ahead, groups), dev),
            device_id_type=pl.DeviceIdType.MESH,
        )
    for ahead in range(1, peers):
        pl.semaphore_signal(
            barrier, inc=1, device_id=(grp, lax.rem(dev + ahead, peers)),
            device_id_type=pl.DeviceIdType.MESH,
        )

    state[0:3, :] = positions[...]
    state[3:6, :] = velocities[...]
    state[6:9, :] = accelerations[...]
    state[9:12, :] = jerks[...]
    state[12:13, :] = -(jnp.left_shift(jnp.int32(1), levels[...]) - 1).astype(F32) * tick_length
    state[13:16, :] = jnp.zeros((3, stars), F32)
    place[3] = jnp.full((slots, 128), soft_sq, F32)

    def send(step, owner, lane, target):
        return pltpu.make_async_remote_copy(
            src_ref=held.at[step, owner],
            dst_ref=held.at[step, owner],
            send_sem=send_sem.at[step, lane],
            recv_sem=recv_sem.at[step, owner],
            device_id=target,
            device_id_type=pl.DeviceIdType.MESH,
        )

    def group_copy(step, ahead):
        return send(step, me, ahead - 1, (lax.rem(grp + ahead, groups), dev))

    def peer_copy(step, back, ahead):
        owner = lax.rem(grp + groups - back, groups) * peers + dev
        lane = (groups - 1) + back * (peers - 1) + ahead - 1
        return send(step, owner, lane, (grp, lax.rem(dev + ahead, peers)))

    def one_step(step, carry):
        now = (step + 1).astype(F32) * tick_length
        span = now - state[12:13, :]
        pred_pos = (
            state[0:3, :]
            + span * state[3:6, :]
            + 0.5 * span * span * state[6:9, :]
            + span * span * span / 6.0 * state[9:12, :]
        )
        pred_vel = state[3:6, :] + span * state[6:9, :] + 0.5 * span * span * state[9:12, :]
        held[step, me, 0:3, :] = pred_pos
        held[step, me, 3:6, :] = pred_vel
        held[step, me, 6:7, :] = jnp.sum(pred_pos * pred_vel, axis=0, keepdims=True)
        held[step, me, 7:8, :] = jnp.ones((1, stars), F32)

        @pl.when(step == 0)
        def _():
            pl.semaphore_wait(barrier, groups + peers - 2)

        for ahead in range(1, groups):
            group_copy(step, ahead).start()
        for ahead in range(1, peers):
            peer_copy(step, 0, ahead).start()

        rows = active_rows[pl.ds(step, 1), :]
        chosen = lax.broadcasted_iota(jnp.int32, (stars, slots), 0) == rows
        chosen = jnp.where(chosen, 1.0, 0.0).astype(BF16)
        values = jnp.concatenate([held[step, me], state[...]], axis=0)
        pieces = jnp.concatenate(split3(values), axis=0).astype(BF16)
        found = jnp.dot(pieces, chosen, preferred_element_type=F32)
        found = found[0:24] + (found[24:48] + found[48:72])
        picked[...] = found
        moved = jnp.concatenate(
            [-found[3:6], -found[0:3], jnp.ones((1, slots), F32), found[6:7]], axis=0
        )
        high, middle, low = split3(moved)
        side = jnp.concatenate(
            [high, middle, low, high, middle, high, found[0:8], jnp.zeros((72, slots), F32)], axis=0
        ).T
        left[...] = side[:, 0:48].astype(BF16)
        for axis in range(3):
            place[axis] = jnp.broadcast_to(side[:, 48 + axis : 49 + axis], (slots, 128))
        total[...] = jnp.zeros_like(total)

        def one_chunk(turn, inner):
            owner_grp = lax.rem(grp + groups - lax.rem(turn, groups), groups)
            owner_dev = lax.rem(dev + peers - turn // groups, peers)
            owner = owner_grp * peers + owner_dev

            @pl.when(turn == 1)
            def _():
                for back in range(1, groups):
                    sender = lax.rem(grp + groups - back, groups) * peers + dev
                    send(step, sender, 0, (grp, lax.rem(dev + 1, peers))).wait_recv()
                    for ahead in range(1, peers):
                        peer_copy(step, back, ahead).start()

            @pl.when(turn >= groups)
            def _():
                send(step, owner, 0, (grp, lax.rem(dev + 1, peers))).wait_recv()

            accumulate(held[step, owner], stars, left, place, total)
            return inner

        lax.fori_loop(0, groups * peers, one_chunk, 0)

        for ahead in range(1, groups):
            group_copy(step, ahead).wait_send()
        for back in range(groups):
            for ahead in range(1, peers):
                peer_copy(step, back, ahead).wait_send()

        sums = total[...]
        direct = sums[0:8] + (sums[8:16] + sums[16:24])
        turned = sums[32:40] + (sums[40:48] + sums[48:56])
        pred = picked[0:8, :]
        force = mass * (direct[0:3] - pred[0:3] * direct[7:8])
        jerk = mass * (
            (direct[3:6] - pred[3:6] * direct[7:8]) - 3.0 * (turned[0:3] - pred[0:3] * turned[7:8])
        )
        old_pos, old_vel = picked[8:11, :], picked[11:14, :]
        old_acc, old_jerk = picked[14:17, :], picked[17:20, :]
        gone = now - picked[20:21, :]
        new_vel = old_vel + 0.5 * gone * (old_acc + force) + gone * gone / 12.0 * (old_jerk - jerk)
        new_pos = old_pos + 0.5 * gone * (old_vel + new_vel) + gone * gone / 12.0 * (old_acc - force)
        picked[0:3, :] = new_pos
        picked[3:6, :] = new_vel
        picked[6:9, :] = force
        picked[9:12, :] = jerk
        picked[12:13, :] = jnp.full((1, slots), now, F32)
        picked[13:14, :] = jnp.ones((1, slots), F32)
        picked[14:16, :] = jnp.zeros((2, slots), F32)
        live = lax.broadcasted_iota(jnp.int32, (1, slots), 1) < counts[step, me]
        pieces = jnp.concatenate(split3(jnp.where(live, picked[0:16, :], 0.0)), axis=0).astype(BF16)
        spread = lax.dot_general(pieces, chosen, NT, preferred_element_type=F32)
        spread = spread[0:16] + (spread[16:32] + spread[32:48])
        state[...] = jnp.where(spread[13:14] > 0.5, spread, state[...])
        return carry

    lax.fori_loop(0, steps, one_step, 0)
    out_pos[...] = state[0:3, :]
    out_vel[...] = state[3:6, :]
    out_acc[...] = state[6:9, :]
    out_jerk[...] = state[9:12, :]


def shards(groups, peers, positions, velocities, accelerations, jerks, levels, counts, active_rows):
    stars = positions.shape[1]
    steps, slots = active_rows.shape
    everyone = groups * peers
    stars_all = stars * everyone
    sends = (groups - 1) + groups * (peers - 1)
    vmem = pl.BlockSpec(memory_space=pltpu.VMEM)
    pairs_all = steps * slots * stars_all
    return pl.pallas_call(
        functools.partial(
            kernel,
            groups,
            peers,
            steps,
            0.0004 * (131072.0 / stars_all) ** (2.0 / 3.0),
            1.0 / stars_all,
        ),
        out_shape=[jax.ShapeDtypeStruct((3, stars), F32)] * 4,
        in_specs=[vmem] * 5 + [pl.BlockSpec(memory_space=pltpu.SMEM), vmem],
        out_specs=[vmem] * 4,
        scratch_shapes=[
            pltpu.VMEM((steps, everyone, 8, stars), F32),
            pltpu.VMEM((16, stars), F32),
            pltpu.VMEM((24, slots), F32),
            pltpu.VMEM((slots, 48), BF16),
            pltpu.VMEM((4, slots, 128), F32),
            pltpu.VMEM((64, slots), F32),
            pltpu.SemaphoreType.DMA((steps, sends)),
            pltpu.SemaphoreType.DMA((steps, everyone)),
        ],
        compiler_params=pltpu.CompilerParams(
            collective_id=0, has_side_effects=True, vmem_limit_bytes=32 * 1024 * 1024
        ),
        cost_estimate=pl.CostEstimate(
            flops=40 * pairs_all, bytes_accessed=64 * stars, transcendentals=pairs_all
        ),
    )(positions, velocities, accelerations, jerks, levels[None, :], counts, active_rows)


def solution(mesh):
    split = P(None, ("grp", "dev"))
    return jax.shard_map(
        functools.partial(shards, mesh.shape["grp"], mesh.shape["dev"]),
        mesh=mesh,
        in_specs=(split, split, split, split, P(("grp", "dev")), P(), split),
        out_specs=(split, split, split, split),
        check_vma=False,
    )
```

```python
import functools

import jax
import jax.numpy as jnp
from jax import lax
from jax.experimental import pallas as pl
from jax.experimental.pallas import tpu as pltpu
from jax.sharding import PartitionSpec as P

tick_length = 1.0 / 128.0
COLS = 256
F32 = jnp.float32
BF16 = jnp.bfloat16
NT = (((1,), (1,)), ((), ()))


def split3(value):
    high = value.astype(BF16).astype(F32)
    rest = value - high
    middle = rest.astype(BF16).astype(F32)
    return high, middle, rest - middle


def add_block(direct, turned, part, pieces):
    sums = [lax.dot_general(part, piece, NT, preferred_element_type=F32) for piece in pieces]
    return direct + sums[0] + sums[1], turned + sums[2] + sums[3]


def accumulate(chunk, width, left_ref, place_ref, total_ref):
    high, middle, low = split3(chunk)
    right = jnp.concatenate([high, high, high, middle, middle, low], axis=0).astype(BF16)
    parts = jnp.concatenate([high, middle, low, jnp.zeros_like(low)], axis=0).astype(BF16)
    direct = total_ref[0:32, :]
    turned = total_ref[32:64, :]
    ready = []
    for start in range(0, width, COLS):
        columns = slice(start, start + COLS)
        mixed = jnp.dot(left_ref[...], right[:, columns], preferred_element_type=F32)
        pieces = [[], [], [], []]
        for lane in range(0, COLS, 128):
            lanes = slice(start + lane, start + lane + 128)
            gap_x = chunk[0:1, lanes] - place_ref[0]
            gap_y = chunk[1:2, lanes] - place_ref[1]
            gap_z = chunk[2:3, lanes] - place_ref[2]
            squared = gap_x * gap_x + gap_y * gap_y + gap_z * gap_z + place_ref[3, 0:1, :]
            inverse = lax.rsqrt(squared)
            twice = inverse * inverse
            weight = twice * inverse
            along = weight * twice * mixed[:, lane : lane + 128]
            weight_high = weight.astype(BF16)
            along_high = along.astype(BF16)
            pieces[0].append(weight_high)
            pieces[1].append((weight - weight_high.astype(F32)).astype(BF16))
            pieces[2].append(along_high)
            pieces[3].append((along - along_high.astype(F32)).astype(BF16))
        ready.append((parts[:, columns], [jnp.concatenate(piece, axis=1) for piece in pieces]))
        if len(ready) > 1:
            direct, turned = add_block(direct, turned, *ready.pop(0))
    direct, turned = add_block(direct, turned, *ready.pop(0))
    total_ref[0:32, :] = direct
    total_ref[32:64, :] = turned


def kernel(
    groups,
    peers,
    steps,
    soft_sq,
    mass,
    positions,
    velocities,
    accelerations,
    jerks,
    levels,
    counts,
    active_rows,
    out_pos,
    out_vel,
    out_acc,
    out_jerk,
    held,
    state,
    picked,
    left,
    place,
    total,
    send_sem,
    recv_sem,
):
    stars = positions.shape[1]
    slots = active_rows.shape[1]
    grp = lax.axis_index("grp")
    dev = lax.axis_index("dev")
    me = grp * peers + dev

    barrier = pltpu.get_barrier_semaphore()
    for ahead in range(1, groups):
        pl.semaphore_signal(
            barrier, inc=1, device_id=(lax.rem(grp + ahead, groups), dev),
            device_id_type=pl.DeviceIdType.MESH,
        )
    for ahead in range(1, peers):
        pl.semaphore_signal(
            barrier, inc=1, device_id=(grp, lax.rem(dev + ahead, peers)),
            device_id_type=pl.DeviceIdType.MESH,
        )

    state[0:3, :] = positions[...]
    state[3:6, :] = velocities[...]
    state[6:9, :] = accelerations[...]
    state[9:12, :] = jerks[...]
    state[12:13, :] = -(jnp.left_shift(jnp.int32(1), levels[...]) - 1).astype(F32) * tick_length
    state[13:16, :] = jnp.zeros((3, stars), F32)
    place[3] = jnp.full((slots, 128), soft_sq, F32)

    def send(step, owner, lane, target):
        return pltpu.make_async_remote_copy(
            src_ref=held.at[step, owner],
            dst_ref=held.at[step, owner],
            send_sem=send_sem.at[step, lane],
            recv_sem=recv_sem.at[step, owner],
            device_id=target,
            device_id_type=pl.DeviceIdType.MESH,
        )

    def group_copy(step, ahead):
        return send(step, me, ahead - 1, (lax.rem(grp + ahead, groups), dev))

    def peer_copy(step, back, ahead):
        owner = lax.rem(grp + groups - back, groups) * peers + dev
        lane = (groups - 1) + back * (peers - 1) + ahead - 1
        return send(step, owner, lane, (grp, lax.rem(dev + ahead, peers)))

    def one_step(step, carry):
        now = (step + 1).astype(F32) * tick_length
        span = now - state[12:13, :]
        pred_pos = (
            state[0:3, :]
            + span * state[3:6, :]
            + 0.5 * span * span * state[6:9, :]
            + span * span * span / 6.0 * state[9:12, :]
        )
        pred_vel = state[3:6, :] + span * state[6:9, :] + 0.5 * span * span * state[9:12, :]
        held[step, me, 0:3, :] = pred_pos
        held[step, me, 3:6, :] = pred_vel
        held[step, me, 6:7, :] = jnp.sum(pred_pos * pred_vel, axis=0, keepdims=True)
        held[step, me, 7:8, :] = jnp.ones((1, stars), F32)

        @pl.when(step == 0)
        def _():
            pl.semaphore_wait(barrier, groups + peers - 2)

        for ahead in range(1, groups):
            group_copy(step, ahead).start()
        for ahead in range(1, peers):
            peer_copy(step, 0, ahead).start()

        rows = active_rows[pl.ds(step, 1), :]
        chosen = lax.broadcasted_iota(jnp.int32, (stars, slots), 0) == rows
        chosen = jnp.where(chosen, 1.0, 0.0).astype(BF16)
        values = jnp.concatenate([held[step, me], state[...]], axis=0)
        pieces = jnp.concatenate(split3(values), axis=0).astype(BF16)
        found = jnp.dot(pieces, chosen, preferred_element_type=F32)
        found = found[0:24] + (found[24:48] + found[48:72])
        picked[...] = found
        moved = jnp.concatenate(
            [-found[3:6], -found[0:3], jnp.ones((1, slots), F32), found[6:7]], axis=0
        )
        high, middle, low = split3(moved)
        side = jnp.concatenate(
            [high, middle, low, high, middle, high, found[0:8], jnp.zeros((72, slots), F32)], axis=0
        ).T
        left[...] = side[:, 0:48].astype(BF16)
        for axis in range(3):
            place[axis] = jnp.broadcast_to(side[:, 48 + axis : 49 + axis], (slots, 128))
        total[...] = jnp.zeros_like(total)

        def one_chunk(turn, inner):
            owner_grp = lax.rem(grp + groups - lax.rem(turn, groups), groups)
            owner_dev = lax.rem(dev + peers - turn // groups, peers)
            owner = owner_grp * peers + owner_dev

            @pl.when(turn == 1)
            def _():
                for back in range(1, groups):
                    sender = lax.rem(grp + groups - back, groups) * peers + dev
                    send(step, sender, 0, (grp, lax.rem(dev + 1, peers))).wait_recv()
                    for ahead in range(1, peers):
                        peer_copy(step, back, ahead).start()

            @pl.when(turn >= groups)
            def _():
                send(step, owner, 0, (grp, lax.rem(dev + 1, peers))).wait_recv()

            accumulate(held[step, owner], stars, left, place, total)
            return inner

        lax.fori_loop(0, groups * peers, one_chunk, 0)

        for ahead in range(1, groups):
            group_copy(step, ahead).wait_send()
        for back in range(groups):
            for ahead in range(1, peers):
                peer_copy(step, back, ahead).wait_send()

        sums = total[...]
        direct = sums[0:8] + (sums[8:16] + sums[16:24])
        turned = sums[32:40] + (sums[40:48] + sums[48:56])
        pred = picked[0:8, :]
        force = mass * (direct[0:3] - pred[0:3] * direct[7:8])
        jerk = mass * (
            (direct[3:6] - pred[3:6] * direct[7:8]) - 3.0 * (turned[0:3] - pred[0:3] * turned[7:8])
        )
        old_pos, old_vel = picked[8:11, :], picked[11:14, :]
        old_acc, old_jerk = picked[14:17, :], picked[17:20, :]
        gone = now - picked[20:21, :]
        new_vel = old_vel + 0.5 * gone * (old_acc + force) + gone * gone / 12.0 * (old_jerk - jerk)
        new_pos = old_pos + 0.5 * gone * (old_vel + new_vel) + gone * gone / 12.0 * (old_acc - force)
        picked[0:3, :] = new_pos
        picked[3:6, :] = new_vel
        picked[6:9, :] = force
        picked[9:12, :] = jerk
        picked[12:13, :] = jnp.full((1, slots), now, F32)
        picked[13:14, :] = jnp.ones((1, slots), F32)
        picked[14:16, :] = jnp.zeros((2, slots), F32)
        live = lax.broadcasted_iota(jnp.int32, (1, slots), 1) < counts[step, me]
        pieces = jnp.concatenate(split3(jnp.where(live, picked[0:16, :], 0.0)), axis=0).astype(BF16)
        spread = lax.dot_general(pieces, chosen, NT, preferred_element_type=F32)
        spread = spread[0:16] + (spread[16:32] + spread[32:48])
        state[...] = jnp.where(spread[13:14] > 0.5, spread, state[...])
        return carry

    lax.fori_loop(0, steps, one_step, 0)
    out_pos[...] = state[0:3, :]
    out_vel[...] = state[3:6, :]
    out_acc[...] = state[6:9, :]
    out_jerk[...] = state[9:12, :]


def shards(groups, peers, positions, velocities, accelerations, jerks, levels, counts, active_rows):
    stars = positions.shape[1]
    steps, slots = active_rows.shape
    everyone = groups * peers
    stars_all = stars * everyone
    sends = (groups - 1) + groups * (peers - 1)
    vmem = pl.BlockSpec(memory_space=pltpu.VMEM)
    pairs_all = steps * slots * stars_all
    return pl.pallas_call(
        functools.partial(
            kernel,
            groups,
            peers,
            steps,
            0.0004 * (131072.0 / stars_all) ** (2.0 / 3.0),
            1.0 / stars_all,
        ),
        out_shape=[jax.ShapeDtypeStruct((3, stars), F32)] * 4,
        in_specs=[vmem] * 5 + [pl.BlockSpec(memory_space=pltpu.SMEM), vmem],
        out_specs=[vmem] * 4,
        scratch_shapes=[
            pltpu.VMEM((steps, everyone, 8, stars), F32),
            pltpu.VMEM((16, stars), F32),
            pltpu.VMEM((24, slots), F32),
            pltpu.VMEM((slots, 48), BF16),
            pltpu.VMEM((4, slots, 128), F32),
            pltpu.VMEM((64, slots), F32),
            pltpu.SemaphoreType.DMA((steps, sends)),
            pltpu.SemaphoreType.DMA((steps, everyone)),
        ],
        compiler_params=pltpu.CompilerParams(
            collective_id=0, has_side_effects=True, vmem_limit_bytes=32 * 1024 * 1024
        ),
        cost_estimate=pl.CostEstimate(
            flops=40 * pairs_all, bytes_accessed=64 * stars, transcendentals=pairs_all
        ),
    )(positions, velocities, accelerations, jerks, levels[None, :], counts, active_rows)


def solution(mesh):
    split = P(None, ("grp", "dev"))
    return jax.shard_map(
        functools.partial(shards, mesh.shape["grp"], mesh.shape["dev"]),
        mesh=mesh,
        in_specs=(split, split, split, split, P(("grp", "dev")), P(), split),
        out_specs=(split, split, split, split),
        check_vma=False,
    )
```
